32 devices in a mesh: groups: 2 (over y), tensor: 2 (over x), expert: 4 (over z), dp: 2 (over core).
Axes of the slice: x: 2, y: 2, z: 4, core: 2. Of those that a mesh axis runs over, the one named last changes fastest.
Arguments:
- tokens: bfloat16 [1024, 6144], P(('groups', 'expert'), ('tensor', 'dp')), parts along dimension 0, may hold values from -6 to 6
- output_gradient: bfloat16 [1024, 6144], P(('groups', 'expert'), ('tensor', 'dp')), parts along dimension 0, may hold values from -6 to 6
- chosen_expert_index: int32 [1024, 2], P(('groups', 'expert')), parts along dimension 0, may hold values from 0 to 3, all different within a row; in each aligned block of 128 rows (0 to 127, 128 to 255, ...) at most 80 rows name the same one
- router_gate_weights: float32 [1024, 2], P(('groups', 'expert')), parts along dimension 0, may hold values from 0.1 to 0.9
- gate_frozen_weight: bfloat16 [4, 6144, 8192], P('expert', None, ('tensor', 'dp')), may hold values from -0.078125 to 0.078125
- up_frozen_weight: bfloat16 [4, 6144, 8192], P('expert', None, ('tensor', 'dp')), may hold values from -0.078125 to 0.078125
- down_frozen_weight: bfloat16 [4, 8192, 6144], P('expert', ('tensor', 'dp')), may hold values from -0.0625 to 0.0625
- gate_adapter_input: bfloat16 [4, 6144, 64], P('expert', ('tensor', 'dp')), may hold values from -0.078125 to 0.078125
- gate_adapter_output: bfloat16 [4, 64, 8192], P('expert', None, ('tensor', 'dp')), may hold values from -0.1796875 to 0.1796875
- up_adapter_input: bfloat16 [4, 6144, 64], P('expert', ('tensor', 'dp')), may hold values from -0.078125 to 0.078125
- up_adapter_output: bfloat16 [4, 64, 8192], P('expert', None, ('tensor', 'dp')), may hold values from -0.1796875 to 0.1796875
- down_adapter_input: bfloat16 [4, 8192, 64], P('expert', ('tensor', 'dp')), may hold values from -0.0625 to 0.0625
- down_adapter_output: bfloat16 [4, 64, 6144], P('expert', None, ('tensor', 'dp')), may hold values from -0.1796875 to 0.1796875
Outputs:
- mixed_out: bfloat16 [1024, 6144], P(('groups', 'expert'), ('tensor', 'dp')), parts along dimension 0
- grad_tokens: bfloat16 [1024, 6144], P(('groups', 'expert'), ('tensor', 'dp')), parts along dimension 0
- prob_grads: float32 [1024, 2], P(('groups', 'expert')), parts along dimension 0
- grad_gate_a: float32 [8, 6144, 64], P(('groups', 'expert'), ('tensor', 'dp')), parts along dimension 0
- grad_gate_b: float32 [8, 64, 8192], P(('groups', 'expert'), None, ('tensor', 'dp')), parts along dimension 0
- grad_up_a: float32 [8, 6144, 64], P(('groups', 'expert'), ('tensor', 'dp')), parts along dimension 0
- grad_up_b: float32 [8, 64, 8192], P(('groups', 'expert'), None, ('tensor', 'dp')), parts along dimension 0
- grad_down_a: float32 [8, 8192, 64], P(('groups', 'expert'), ('tensor', 'dp')), parts along dimension 0
- grad_down_b: float32 [8, 64, 6144], P(('groups', 'expert'), None, ('tensor', 'dp')), parts along dimension 0
The draws below stay inside these ranges and needn't reach their ends.
There are 2 independent parts, one for each index of `groups`. The reference program is written for one: setup_inputs(seed, part) draws one part's arguments, and reference() takes and returns one part's arrays. A program takes and returns all parts, laid end to end along the dimension named above; an argument that names none is the same for every part. Nothing has to cross between parts.
Inputs may be any that keep to these rules, and one draw needn't show every extreme that they name: `chosen_expert_index`: each token names two different experts. Among the 128 tokens of one aligned block, no expert is named by more than 80 tokens, and in some block some expert is named by exactly 80.
All inputs are finite; a program needn't handle non-finite values.
Results may differ from the reference program's by a relative error of at most 0.007.
Values may be sent and summed in bfloat16 or wider, within the bound.
A program may use at most 256 MiB of HBM per device.

```python
import math
import jax
import jax.numpy as jnp
import numpy as np
from jax import lax

MODEL_WIDTH = 6144
HIDDEN_SLICE = 8192
ADAPTER_RANK = 64
TOK_DEV = 128
EXPERT_COUNT = 4
TOKENS = 512
CAP = 80
N_EXPERT = 4


def block_levels(stream_key, extent, pieces, smallest, high):
    gain = 1.0
    for dim, blocks in pieces:
        heights = jax.random.uniform(jax.random.fold_in(jax.random.fold_in(stream_key, 6), dim), (blocks,), jnp.float32, smallest / len(pieces), high / len(pieces))
        gain = gain * jnp.repeat(jnp.exp(heights), extent[dim] // blocks).reshape((-1,) + (1,) * (len(extent) - 1 - dim))
    return gain


def deal_out(own_key, own, number, rows, number_of, top, limit, lean):
    sequence = jax.random.permutation(own_key, number_of)
    heavy_load, usual = load_shares(number_of, rows * top, limit, lean, True), load_shares(number_of, rows * top, limit, lean, False)
    places = jnp.arange(number_of)

    def named(sizes, rotation):
        used = int((sizes > 0).sum())
        fixed = max(1, used // 4)
        moved = fixed + (places - fixed + rotation * (used - fixed)) % max(1, number_of - fixed)
        return jnp.zeros((number_of,), jnp.int32).at[sequence[jnp.where(places < fixed, places, moved)]].set(jnp.asarray(sizes, jnp.int32))

    sizes = jnp.where(number % 4 == 0, named(heavy_load, number // 4), named(usual, number - number // 4 - 1))
    mixed = jax.random.permutation(jax.random.fold_in(own, 3), number_of)
    giver, taker = mixed[0:number_of // 2 * 2:2], mixed[1:number_of // 2 * 2:2]
    room = jnp.minimum(sizes[giver] - 1, limit - sizes[taker]) // 2
    room = jnp.where((giver == sequence[0]) | (taker == sequence[0]) | (sizes[taker] == 0), 0, jnp.maximum(room, 0))
    moved = jax.random.randint(jax.random.fold_in(own, 4), (number_of // 2,), 0, 1 << 20) % (room + 1)
    sizes = sizes.at[giver].add(-moved).at[taker].add(moved)
    members = jnp.searchsorted(jnp.cumsum(sizes), jnp.arange(rows * top), side="right").astype(jnp.int32)
    listing = members.reshape(top, rows).T
    listing = listing[jax.random.permutation(jax.random.fold_in(own, 1), rows)]
    rotation = jax.random.randint(jax.random.fold_in(own, 2), (rows, 1), 0, top)
    return jnp.take_along_axis(listing, (jnp.arange(top)[None, :] + rotation) % top, axis=1)


def load_shares(amount, total, reach, lean, full):
    loads = [(1 << 20) // math.isqrt(rank ** lean) + 1 for rank in range(1, amount + 1)]
    largest = reach if full else min(reach, max(-(-total // amount), total * loads[0] // sum(loads)))
    least = 1 if total - largest >= amount - 1 else 0
    holding, surplus = [largest] + [least] * (amount - 1), total - largest - least * (amount - 1)
    while surplus > 0:
        candidates = [i for i in range(1, amount) if holding[i] < largest] or [i for i in range(1, amount) if holding[i] < reach]
        pool, remaining = sum([loads[i] for i in candidates]), surplus
        for i in candidates:
            addition = min(reach - holding[i], max(1, remaining * loads[i] // pool), surplus)
            holding[i] = holding[i] + addition
            surplus = surplus - addition
    return np.array(holding)


def centred(key, dims, width, limit, cuts=(), kind=jnp.bfloat16):
    entries = jax.random.normal(key, dims, jnp.float32) * width
    if len(cuts) > 0:
        entries = block_levels(key, dims, cuts, -0.22, 0.18) * entries
    return jnp.clip(entries, min=-limit, max=limit).astype(kind)


def setup_inputs(seed: int = 0, part: int = 0) -> dict:
    keys = jax.random.split(jax.random.key(seed), 14)
    part_splits = jax.random.split(jax.random.fold_in(keys[13], part), 14)
    tokens = centred(part_splits[0], (TOKENS, MODEL_WIDTH), 1.0, 6.0, ((0, 4), (1, 4)))
    output_gradient = centred(part_splits[1], (TOKENS, MODEL_WIDTH), 1.0, 6.0, ((0, 4), (1, 4)))
    chosen_expert_index_keys = jax.random.split(jax.random.fold_in(part_splits[2], 1), TOKENS // TOK_DEV)
    chosen_expert_index_turns = jax.random.permutation(jax.random.fold_in(part_splits[2], 3), TOKENS // TOK_DEV)
    chosen_expert_index = jax.vmap(lambda own, number: deal_out(jax.random.fold_in(part_splits[2], 2), own, number, TOK_DEV, EXPERT_COUNT, 2, CAP, 2))(chosen_expert_index_keys, chosen_expert_index_turns).reshape((TOKENS, 2))
    router_gate_weights = jnp.clip(0.1 + 0.79999997 * jax.random.uniform(part_splits[3], (TOKENS, 2), jnp.float32) ** block_levels(part_splits[3], (TOKENS, 2), ((0, 4),), -0.2, 0.2), 0.1, 0.9)
    gate_frozen_weight = centred(keys[4], (EXPERT_COUNT, MODEL_WIDTH, HIDDEN_SLICE), MODEL_WIDTH ** -0.5, 0.078125, ((0, 4), (2, 4)))
    up_frozen_weight = centred(keys[5], (EXPERT_COUNT, MODEL_WIDTH, HIDDEN_SLICE), MODEL_WIDTH ** -0.5, 0.078125, ((0, 4), (2, 4)))
    down_frozen_weight = centred(keys[6], (EXPERT_COUNT, HIDDEN_SLICE, MODEL_WIDTH), HIDDEN_SLICE ** -0.5, 0.0625, ((0, 4), (1, 4)))
    gate_adapter_input = centred(keys[7], (EXPERT_COUNT, MODEL_WIDTH, ADAPTER_RANK), MODEL_WIDTH ** -0.5, 0.078125, ((0, 4), (1, 4)))
    gate_adapter_output = centred(keys[8], (EXPERT_COUNT, ADAPTER_RANK, HIDDEN_SLICE), 0.03, 0.1796875, ((0, 4), (2, 4)))
    up_adapter_input = centred(keys[9], (EXPERT_COUNT, MODEL_WIDTH, ADAPTER_RANK), MODEL_WIDTH ** -0.5, 0.078125, ((0, 4), (1, 4)))
    up_adapter_output = centred(keys[10], (EXPERT_COUNT, ADAPTER_RANK, HIDDEN_SLICE), 0.03, 0.1796875, ((0, 4), (2, 4)))
    down_adapter_input = centred(keys[11], (EXPERT_COUNT, HIDDEN_SLICE, ADAPTER_RANK), HIDDEN_SLICE ** -0.5, 0.0625, ((0, 4), (1, 4)))
    down_adapter_output = centred(keys[12], (EXPERT_COUNT, ADAPTER_RANK, MODEL_WIDTH), 0.03, 0.1796875, ((0, 4), (2, 4)))
    return dict(tokens=tokens, output_gradient=output_gradient, chosen_expert_index=chosen_expert_index, router_gate_weights=router_gate_weights, gate_frozen_weight=gate_frozen_weight, up_frozen_weight=up_frozen_weight, down_frozen_weight=down_frozen_weight, gate_adapter_input=gate_adapter_input, gate_adapter_output=gate_adapter_output, up_adapter_input=up_adapter_input, up_adapter_output=up_adapter_output, down_adapter_input=down_adapter_input, down_adapter_output=down_adapter_output)


adapter_scale = 2.0


def contract_matrices(left_op, right_op, left_dim, right_dim):
    return lax.dot_general(left_op, right_op, (((left_dim,), (right_dim,)), ((), ())), preferred_element_type=jnp.float32)


def silu_parts(gate_preactivation):
    sig_val = jax.nn.sigmoid(gate_preactivation)
    return gate_preactivation * sig_val, sig_val * (1.0 + gate_preactivation * (1.0 - sig_val))


def reference(tokens, output_gradient, chosen_expert_index, router_gate_weights, gate_frozen_weight, up_frozen_weight, down_frozen_weight, gate_adapter_input, gate_adapter_output, up_adapter_input, up_adapter_output, down_adapter_input, down_adapter_output):
    sources = N_EXPERT
    grouped = chosen_expert_index.reshape(sources, TOK_DEV * 2)
    hit_mask = (grouped[:, :, None] == jnp.arange(EXPERT_COUNT, dtype=jnp.int32)[None, None, :]).astype(jnp.int32)
    before = jnp.cumsum(hit_mask, axis=1) - hit_mask
    slot_num = jnp.sum(before * hit_mask, axis=2)
    position = (jnp.arange(sources, dtype=jnp.int32)[:, None] * CAP + slot_num).reshape(-1).astype(jnp.int32)
    owner = chosen_expert_index.reshape(-1).astype(jnp.int32)
    token_of = (jnp.arange(TOKENS * 2, dtype=jnp.int32) // 2).astype(jnp.int32)
    probs_flat = router_gate_weights.reshape(-1, 1)
    buffer_rows = sources * CAP
    empty_buf = jnp.zeros((EXPERT_COUNT, buffer_rows, MODEL_WIDTH), jnp.bfloat16)
    x_buf = empty_buf.at[owner, position].set(tokens[token_of])
    t_rows = (output_gradient[token_of].astype(jnp.float32) * probs_flat).astype(jnp.bfloat16)
    t_buf = empty_buf.at[owner, position].set(t_rows)
    out_list = []
    dx_list = []
    gradient_collections = [[], [], [], [], [], []]
    for expert_number in range(EXPERT_COUNT):
        input_rows = x_buf[expert_number]
        token_full_rows = t_buf[expert_number]
        gate_rank_codes = contract_matrices(input_rows, gate_adapter_input[expert_number], 1, 0).astype(jnp.bfloat16)
        up_rank_codes = contract_matrices(input_rows, up_adapter_input[expert_number], 1, 0).astype(jnp.bfloat16)
        gate_preactivation = contract_matrices(input_rows, gate_frozen_weight[expert_number], 1, 0) + adapter_scale * contract_matrices(gate_rank_codes, gate_adapter_output[expert_number], 1, 0)
        up_preactivation = contract_matrices(input_rows, up_frozen_weight[expert_number], 1, 0) + adapter_scale * contract_matrices(up_rank_codes, up_adapter_output[expert_number], 1, 0)
        silu_val, silu_grad = silu_parts(gate_preactivation)
        hidden_activation = (silu_val * up_preactivation).astype(jnp.bfloat16)
        down_rank_codes = contract_matrices(hidden_activation, down_adapter_input[expert_number], 1, 0).astype(jnp.bfloat16)
        output_rows = (contract_matrices(hidden_activation, down_frozen_weight[expert_number], 1, 0) + adapter_scale * contract_matrices(down_rank_codes, down_adapter_output[expert_number], 1, 0)).astype(jnp.bfloat16)
        backward_down_codes = (adapter_scale * contract_matrices(token_full_rows, down_adapter_output[expert_number], 1, 1)).astype(jnp.bfloat16)
        hidden_gradient = contract_matrices(token_full_rows, down_frozen_weight[expert_number], 1, 1) + contract_matrices(backward_down_codes, down_adapter_input[expert_number], 1, 1)
        gate_preact_gradient = (hidden_gradient * up_preactivation * silu_grad).astype(jnp.bfloat16)
        up_preact_gradient = (hidden_gradient * silu_val).astype(jnp.bfloat16)
        backward_gate_codes = (adapter_scale * contract_matrices(gate_preact_gradient, gate_adapter_output[expert_number], 1, 1)).astype(jnp.bfloat16)
        backward_up_codes = (adapter_scale * contract_matrices(up_preact_gradient, up_adapter_output[expert_number], 1, 1)).astype(jnp.bfloat16)
        input_gradient_rows = contract_matrices(gate_preact_gradient, gate_frozen_weight[expert_number], 1, 1) + contract_matrices(up_preact_gradient, up_frozen_weight[expert_number], 1, 1)
        input_gradient_rows = input_gradient_rows + contract_matrices(backward_gate_codes, gate_adapter_input[expert_number], 1, 1) + contract_matrices(backward_up_codes, up_adapter_input[expert_number], 1, 1)
        out_list.append(output_rows)
        dx_list.append(input_gradient_rows.astype(jnp.bfloat16))
        gradient_collections[0].append(contract_matrices(input_rows, backward_gate_codes, 0, 0))
        gradient_collections[1].append(adapter_scale * contract_matrices(gate_rank_codes, gate_preact_gradient, 0, 0))
        gradient_collections[2].append(contract_matrices(input_rows, backward_up_codes, 0, 0))
        gradient_collections[3].append(adapter_scale * contract_matrices(up_rank_codes, up_preact_gradient, 0, 0))
        gradient_collections[4].append(contract_matrices(hidden_activation, backward_down_codes, 0, 0))
        gradient_collections[5].append(adapter_scale * contract_matrices(down_rank_codes, token_full_rows, 0, 0))
    out_buf = jnp.stack(out_list)
    dx_buf = jnp.stack(dx_list)
    out_pairs = out_buf[owner, position].astype(jnp.float32).reshape(TOKENS, 2, MODEL_WIDTH)
    mixed_out = jnp.sum(out_pairs * router_gate_weights[:, :, None], axis=1).astype(jnp.bfloat16)
    prob_grads = jnp.sum(out_pairs * output_gradient[:, None, :].astype(jnp.float32), axis=2)
    dx_pairs = dx_buf[owner, position].astype(jnp.float32).reshape(TOKENS, 2, MODEL_WIDTH)
    grad_tokens = jnp.sum(dx_pairs, axis=1).astype(jnp.bfloat16)
    return (mixed_out, grad_tokens, prob_grads, jnp.stack(gradient_collections[0]), jnp.stack(gradient_collections[1]), jnp.stack(gradient_collections[2]), jnp.stack(gradient_collections[3]), jnp.stack(gradient_collections[4]), jnp.stack(gradient_collections[5]))
```

```python
import jax
import jax.numpy as jnp
from jax import lax
from jax.experimental import pallas as pl
from jax.experimental.pallas import tpu as pltpu
from jax.sharding import PartitionSpec as P

adapter_scale = 2.0


def contract_matrices(left_op, right_op, left_dim, right_dim):
    return lax.dot_general(
        left_op,
        right_op,
        (((left_dim,), (right_dim,)), ((), ())),
        preferred_element_type=jnp.float32,
    )


def silu_parts(gate_preactivation):
    sig_val = jax.nn.sigmoid(gate_preactivation)
    return (gate_preactivation * sig_val, sig_val * (1.0 + gate_preactivation * (1.0 - sig_val)))


def build_table(chosen_expert_index, experts, capacity):
    flat_ids = chosen_expert_index.reshape(-1)
    hit_mask = (flat_ids[:, None] == jnp.arange(experts, dtype=jnp.int32)[None, :]).astype(
        jnp.int32
    )
    before = jnp.cumsum(hit_mask, axis=0) - hit_mask
    slot_num = jnp.sum(before * hit_mask, axis=1)
    target = flat_ids * capacity + slot_num
    return (target[:, None] == jnp.arange(experts * capacity, dtype=jnp.int32)[None, :]).astype(
        jnp.bfloat16
    )


def collect(results, slot_map, experts, capacity):
    returned = lax.all_to_all(
        results.reshape(experts, capacity, -1), "expert", split_axis=0, concat_axis=0, tiled=True
    )
    return contract_matrices(slot_map, returned.reshape(experts * capacity, -1), 1, 0)


def expert_forward(
    input_full_rows,
    gate_weight_matrix,
    up_weight_matrix,
    gate_output_factor,
    up_output_factor,
    gate_rank_codes,
    up_rank_codes,
):
    gate_preactivation = contract_matrices(
        input_full_rows, gate_weight_matrix, 1, 0
    ) + adapter_scale * contract_matrices(gate_rank_codes, gate_output_factor, 1, 0)
    up_preactivation = contract_matrices(
        input_full_rows, up_weight_matrix, 1, 0
    ) + adapter_scale * contract_matrices(up_rank_codes, up_output_factor, 1, 0)
    silu_val, silu_grad = silu_parts(gate_preactivation)
    hidden_activation = (silu_val * up_preactivation).astype(jnp.bfloat16)
    return (up_preactivation, silu_val, silu_grad, hidden_activation)


def expert_backward(
    token_full_rows,
    backward_down_codes,
    down_weight_matrix,
    down_input_factor,
    gate_weight_matrix,
    up_weight_matrix,
    gate_output_factor,
    up_output_factor,
    up_preactivation,
    silu_val,
    silu_grad,
):
    hidden_gradient = contract_matrices(
        token_full_rows, down_weight_matrix, 1, 1
    ) + contract_matrices(backward_down_codes, down_input_factor, 1, 1)
    gate_preact_gradient = (hidden_gradient * up_preactivation * silu_grad).astype(jnp.bfloat16)
    up_preact_gradient = (hidden_gradient * silu_val).astype(jnp.bfloat16)
    dx_terms = contract_matrices(
        gate_preact_gradient, gate_weight_matrix, 1, 1
    ) + contract_matrices(up_preact_gradient, up_weight_matrix, 1, 1)
    code_terms = (
        contract_matrices(gate_preact_gradient, gate_output_factor, 1, 1),
        contract_matrices(up_preact_gradient, up_output_factor, 1, 1),
    )
    return (gate_preact_gradient, up_preact_gradient, dx_terms, code_terms)


def flat_sum(partial_terms, extra_term):
    main_sum = lax.psum_scatter(partial_terms, ("tensor", "dp"), scatter_dimension=1, tiled=True)
    return (main_sum + extra_term).astype(jnp.bfloat16)


vmem_bytes = 48 * 1024 * 1024


def nn(left_op, right_op):
    return contract_matrices(left_op, right_op, 1, 0)


def nt(left_op, right_op):
    return contract_matrices(left_op, right_op, 1, 1)


def call_tiles(body, tiles, order, operands, in_specs, out_shape, out_specs, flops, moved):
    return pl.pallas_call(
        body,
        grid_spec=pltpu.PrefetchScalarGridSpec(
            num_scalar_prefetch=1, grid=(tiles,), in_specs=in_specs, out_specs=out_specs
        ),
        out_shape=out_shape,
        compiler_params=pltpu.CompilerParams(vmem_limit_bytes=vmem_bytes),
        cost_estimate=pl.CostEstimate(flops=flops, bytes_accessed=moved, transcendentals=0),
    )(order, *operands)


def whole(arr):
    return pl.BlockSpec(arr.shape, lambda n, order: (0, 0))


def forward_tiles(order, pieces, gate_w, up_w, gate_codes, up_codes, gate_b, up_b, tile=256):
    rows, width = pieces[0].shape
    hidden = gate_w.shape[1]
    parts = len(pieces)

    def body(order_ref, *refs):
        xs, gs, us = refs[:parts], refs[parts : 2 * parts], refs[2 * parts : 3 * parts]
        gc, uc, gb, ub, hid_ref, up_ref, val_ref = refs[3 * parts :]
        gate = adapter_scale * nn(gc[...], gb[...])
        up = adapter_scale * nn(uc[...], ub[...])
        for x_ref, g_ref in zip(xs, gs):
            gate += nn(x_ref[...], g_ref[...])
        for x_ref, u_ref in zip(xs, us):
            up += nn(x_ref[...], u_ref[...])
        val, grad = silu_parts(gate)
        hid_ref[...] = (val * up).astype(jnp.bfloat16)
        up_ref[...] = up * grad
        val_ref[...] = val

    def weight(k):
        return pl.BlockSpec((width, tile), lambda n, order: (order[k], n))

    def column(arr):
        return pl.BlockSpec((arr.shape[0], tile), lambda n, order: (0, n))

    out = pl.BlockSpec((rows, tile), lambda n, order: (0, n))
    return call_tiles(
        body,
        hidden // tile,
        order,
        (*pieces, *[gate_w] * parts, *[up_w] * parts, gate_codes, up_codes, gate_b, up_b),
        [whole(p) for p in pieces]
        + [weight(k) for k in range(parts)] * 2
        + [whole(gate_codes), whole(up_codes), column(gate_b), column(up_b)],
        (
            jax.ShapeDtypeStruct((rows, hidden), jnp.bfloat16),
            jax.ShapeDtypeStruct((rows, hidden), jnp.float32),
            jax.ShapeDtypeStruct((rows, hidden), jnp.float32),
        ),
        (out, out, out),
        4 * rows * width * parts * hidden,
        4 * width * parts * hidden,
    )


def backward_tiles(order, pieces, down_w, codes, down_a, up_term, silu_val, tile=256):
    rows, width = pieces[0].shape
    hidden = down_w.shape[0]
    parts = len(pieces)

    def body(order_ref, *refs):
        ts, ws = refs[:parts], refs[parts : 2 * parts]
        bc, da, up_ref, val_ref, dg_ref, du_ref = refs[2 * parts :]
        grad = nt(bc[...], da[...])
        for t_ref, w_ref in zip(ts, ws):
            grad += nt(t_ref[...], w_ref[...])
        dg_ref[...] = (grad * up_ref[...]).astype(jnp.bfloat16)
        du_ref[...] = (grad * val_ref[...]).astype(jnp.bfloat16)

    def weight(k):
        return pl.BlockSpec((tile, width), lambda n, order: (n, order[k]))

    out = pl.BlockSpec((rows, tile), lambda n, order: (0, n))
    return call_tiles(
        body,
        hidden // tile,
        order,
        (*pieces, *[down_w] * parts, codes, down_a, up_term, silu_val),
        [whole(p) for p in pieces]
        + [weight(k) for k in range(parts)]
        + [whole(codes), pl.BlockSpec((tile, down_a.shape[1]), lambda n, order: (n, 0)), out, out],
        (jax.ShapeDtypeStruct((rows, hidden), jnp.bfloat16),) * 2,
        (out, out),
        2 * rows * width * parts * hidden,
        2 * width * parts * hidden,
    )


def feature_piece(order, k, left, weights, transposed, width, added, kind, tile):
    rows, hidden = left[0].shape
    count = len(left)
    steps = width // tile

    def body(order_ref, *refs):
        total = None
        for l_ref, w_ref in zip(refs[:count], refs[count : 2 * count]):
            term = (nt if transposed else nn)(l_ref[...], w_ref[...])
            total = term if total is None else total + term
        if added is not None:
            total = total + refs[2 * count][...].astype(jnp.float32)
        refs[-1][...] = total.astype(kind)

    out = pl.BlockSpec((rows, tile), lambda n, order: (0, n))
    if transposed:
        weight = pl.BlockSpec((tile, hidden), lambda n, order: (order[k] * steps + n, 0))
    else:
        weight = pl.BlockSpec((hidden, tile), lambda n, order: (0, order[k] * steps + n))
    extra = () if added is None else (added,)
    return call_tiles(
        body,
        steps,
        order,
        (*left, *weights, *extra),
        [whole(a) for a in left] + [weight] * count + [out] * len(extra),
        jax.ShapeDtypeStruct((rows, width), kind),
        out,
        2 * rows * hidden * width * count,
        2 * hidden * width * count,
    )


def swap(arr, axis):
    return lax.ppermute(arr, axis, [(0, 1), (1, 0)])


def sum_pairs(arr):
    arr = arr + swap(arr, "dp")
    return arr + swap(arr, "tensor")


def rotate(arr, shift, experts):
    if shift % experts == 0:
        return arr
    return lax.ppermute(arr, "expert", [(e, (e + shift) % experts) for e in range(experts)])


def quad_device(
    tokens,
    output_gradient,
    chosen_expert_index,
    router_gate_weights,
    gate_frozen_weight,
    up_frozen_weight,
    down_frozen_weight,
    gate_adapter_input,
    gate_adapter_output,
    up_adapter_input,
    up_adapter_output,
    down_adapter_input,
    down_adapter_output,
):
    experts = lax.axis_size("expert")
    me = lax.axis_index("expert")
    tok_count, width = tokens.shape
    capacity = max(5 * tok_count // 8, 2 * tok_count // experts)
    buffer_rows = experts * capacity
    far, near = lax.axis_index("tensor"), lax.axis_index("dp")
    order = jnp.stack(
        [2 * far + near, 2 * far + 1 - near, 2 * (1 - far) + near, 2 * (1 - far) + 1 - near]
    ).astype(jnp.int32)
    gate_w, up_w, down_w = gate_frozen_weight[0], up_frozen_weight[0], down_frozen_weight[0]
    gate_a, up_a, down_a = gate_adapter_input[0], up_adapter_input[0], down_adapter_input[0]
    gate_b, up_b, down_b = gate_adapter_output[0], up_adapter_output[0], down_adapter_output[0]

    hits = [
        chosen_expert_index[:, k : k + 1] == jnp.arange(experts, dtype=jnp.int32)[None, :]
        for k in range(2)
    ]
    both = (hits[0] | hits[1]).astype(jnp.bfloat16)
    place = jnp.arange(tok_count, dtype=jnp.int32)
    earlier = (place[:, None] > place[None, :]).astype(jnp.bfloat16)
    before = nn(earlier, both).astype(jnp.int32)
    slot_maps = []
    for k in range(2):
        slot_num = jnp.sum(jnp.where(hits[k], before, 0), axis=1)
        turned = lax.rem(chosen_expert_index[:, k] - me + experts, experts)
        target = turned * capacity + slot_num
        slot_maps.append(
            (target[:, None] == jnp.arange(buffer_rows, dtype=jnp.int32)[None, :]).astype(
                jnp.bfloat16
            )
        )
    token_map = slot_maps[0] + slot_maps[1]
    gradient_wide = output_gradient.astype(jnp.float32)
    probs = [router_gate_weights[:, k : k + 1] for k in range(2)]

    def dispatch(buf):
        cut = [buf[s * capacity : (s + 1) * capacity] for s in range(experts)]
        own = [rotate(cut[s], s, experts) for s in range(experts)]
        other = [swap(block, "tensor") for block in own]
        own, other = jnp.concatenate(own), jnp.concatenate(other)
        return (own, swap(own, "dp"), other, swap(other, "dp"))

    x_buf = contract_matrices(token_map, tokens, 0, 0).astype(jnp.bfloat16)
    t_buf = (
        contract_matrices(slot_maps[0], (gradient_wide * probs[0]).astype(jnp.bfloat16), 0, 0)
        + contract_matrices(slot_maps[1], (gradient_wide * probs[1]).astype(jnp.bfloat16), 0, 0)
    ).astype(jnp.bfloat16)
    x_pieces = dispatch(x_buf)
    t_pieces = dispatch(t_buf)
    x_part, t_part = x_pieces[0], t_pieces[0]
    codes = sum_pairs(nn(x_part, jnp.concatenate([gate_a, up_a], axis=1))).astype(jnp.bfloat16)
    rank = gate_a.shape[1]
    gate_codes, up_codes = codes[:, :rank], codes[:, rank:]
    back_down = (adapter_scale * sum_pairs(nt(t_part, down_b))).astype(jnp.bfloat16)

    hidden_act, up_term, silu_val = forward_tiles(
        order, x_pieces, gate_w, up_w, gate_codes, up_codes, gate_b, up_b
    )

    def scatter_sum(left, weights, transposed, tile):
        def piece(k, added, kind):
            return feature_piece(order, k, left, weights, transposed, width, added, kind, tile)

        to_both = swap(piece(3, None, jnp.bfloat16), "dp")
        to_core = swap(piece(1, None, jnp.bfloat16), "dp")
        to_chip = piece(2, to_both, jnp.bfloat16)
        kept = piece(0, to_core, jnp.float32)
        return kept, to_chip

    def send_back(kept, to_chip, extra):
        sequence = [2 % experts] + [s for s in range(experts - 1, 0, -1) if s != 2] + [0]
        arrived = {}
        for s in dict.fromkeys(sequence):
            cut = slice(s * capacity, (s + 1) * capacity)
            block = (kept[cut] + extra[cut] + swap(to_chip[cut], "tensor").astype(jnp.float32))
            arrived[s] = rotate(block.astype(jnp.bfloat16), -s, experts)
        return jnp.concatenate([arrived[s] for s in range(experts)])

    out_kept, out_chip = scatter_sum((hidden_act,), (down_w,), False, 512)
    down_codes = sum_pairs(nn(hidden_act, down_a)).astype(jnp.bfloat16)
    out_back = send_back(out_kept, out_chip, adapter_scale * nn(down_codes, down_b))

    d_gate, d_up = backward_tiles(order, t_pieces, down_w, back_down, down_a, up_term, silu_val)
    dx_kept, dx_chip = scatter_sum((d_gate, d_up), (gate_w, up_w), True, 256)
    back_codes = adapter_scale * sum_pairs(
        jnp.concatenate([nt(d_gate, gate_b), nt(d_up, up_b)], axis=1)
    )
    back_codes = back_codes.astype(jnp.bfloat16)
    back_gate, back_up = back_codes[:, :rank], back_codes[:, rank:]
    dx_back = send_back(dx_kept, dx_chip, nt(back_gate, gate_a) + nt(back_up, up_a))

    grad_codes = contract_matrices(x_part, back_codes, 0, 0)
    grad_list = (
        grad_codes[:, :rank],
        adapter_scale * contract_matrices(gate_codes, d_gate, 0, 0),
        grad_codes[:, rank:],
        adapter_scale * contract_matrices(up_codes, d_up, 0, 0),
        contract_matrices(hidden_act, back_down, 0, 0),
        adapter_scale * contract_matrices(down_codes, t_part, 0, 0),
    )
    rows_out = [nn(slot_maps[k], out_back) for k in range(2)]
    mixed_out = (rows_out[0] * probs[0] + rows_out[1] * probs[1]).astype(jnp.bfloat16)
    prob_grads = sum_pairs(
        jnp.stack([jnp.sum(rows_out[k] * gradient_wide, axis=1) for k in range(2)], axis=1)
    )
    grad_tokens = nn(token_map, dx_back).astype(jnp.bfloat16)
    return (mixed_out, grad_tokens, prob_grads, *[g[None] for g in grad_list])


def per_device(
    tokens,
    output_gradient,
    chosen_expert_index,
    router_gate_weights,
    gate_frozen_weight,
    up_frozen_weight,
    down_frozen_weight,
    gate_adapter_input,
    gate_adapter_output,
    up_adapter_input,
    up_adapter_output,
    down_adapter_input,
    down_adapter_output,
):
    experts = lax.axis_size("expert")
    tok_count = tokens.shape[0]
    capacity = max(5 * tok_count // 8, 2 * tok_count // experts)
    buffer_rows = experts * capacity
    slot_map = build_table(chosen_expert_index, experts, capacity)
    probs_flat = router_gate_weights.reshape(-1, 1)
    gate_weight_matrix = gate_frozen_weight[0]
    up_weight_matrix = up_frozen_weight[0]
    down_weight_matrix = down_frozen_weight[0]
    gate_input_factor = gate_adapter_input[0]
    gate_output_factor = gate_adapter_output[0]
    up_input_factor = up_adapter_input[0]
    up_output_factor = up_adapter_output[0]
    down_input_factor = down_adapter_input[0]
    down_output_factor = down_adapter_output[0]
    t_rows = (jnp.repeat(output_gradient, 2, axis=0).astype(jnp.float32) * probs_flat).astype(
        jnp.bfloat16
    )
    x_buf = (
        contract_matrices(slot_map, jnp.repeat(tokens, 2, axis=0), 0, 0)
        .astype(jnp.bfloat16)
        .reshape(experts, capacity, -1)
    )
    t_buf = (
        contract_matrices(slot_map, t_rows, 0, 0)
        .astype(jnp.bfloat16)
        .reshape(experts, capacity, -1)
    )
    x_arrived, t_arrived = (
        lax.all_to_all(x_buf, "expert", split_axis=0, concat_axis=0, tiled=True),
        lax.all_to_all(t_buf, "expert", split_axis=0, concat_axis=0, tiled=True),
    )
    x_part = x_arrived.reshape(buffer_rows, -1)
    token_partial_rows = t_arrived.reshape(buffer_rows, -1)
    rank_code_totals = lax.psum(
        (
            contract_matrices(x_part, gate_input_factor, 1, 0),
            contract_matrices(x_part, up_input_factor, 1, 0),
            contract_matrices(token_partial_rows, down_output_factor, 1, 1),
        ),
        ("tensor", "dp"),
    )
    gate_rank_codes = rank_code_totals[0].astype(jnp.bfloat16)
    up_rank_codes = rank_code_totals[1].astype(jnp.bfloat16)
    backward_down_codes = (adapter_scale * rank_code_totals[2]).astype(jnp.bfloat16)
    input_full_rows, token_full_rows = (
        lax.all_gather(x_part, ("tensor", "dp"), axis=1, tiled=True),
        lax.all_gather(token_partial_rows, ("tensor", "dp"), axis=1, tiled=True),
    )
    up_preactivation, silu_val, silu_grad, hidden_activation = expert_forward(
        input_full_rows,
        gate_weight_matrix,
        up_weight_matrix,
        gate_output_factor,
        up_output_factor,
        gate_rank_codes,
        up_rank_codes,
    )
    down_rank_codes = lax.psum(
        contract_matrices(hidden_activation, down_input_factor, 1, 0), ("tensor", "dp")
    ).astype(jnp.bfloat16)
    out_part = flat_sum(
        contract_matrices(hidden_activation, down_weight_matrix, 1, 0),
        adapter_scale * contract_matrices(down_rank_codes, down_output_factor, 1, 0),
    )
    gate_preact_gradient, up_preact_gradient, dx_terms, code_terms = expert_backward(
        token_full_rows,
        backward_down_codes,
        down_weight_matrix,
        down_input_factor,
        gate_weight_matrix,
        up_weight_matrix,
        gate_output_factor,
        up_output_factor,
        up_preactivation,
        silu_val,
        silu_grad,
    )
    backward_rank_codes = lax.psum((code_terms[0], code_terms[1]), ("tensor", "dp"))
    gate_code_gradient = (adapter_scale * backward_rank_codes[0]).astype(jnp.bfloat16)
    up_code_gradient = (adapter_scale * backward_rank_codes[1]).astype(jnp.bfloat16)
    dx_part = flat_sum(
        dx_terms,
        contract_matrices(gate_code_gradient, gate_input_factor, 1, 1)
        + contract_matrices(up_code_gradient, up_input_factor, 1, 1),
    )
    grad_list = (
        contract_matrices(x_part, gate_code_gradient, 0, 0),
        adapter_scale * contract_matrices(gate_rank_codes, gate_preact_gradient, 0, 0),
        contract_matrices(x_part, up_code_gradient, 0, 0),
        adapter_scale * contract_matrices(up_rank_codes, up_preact_gradient, 0, 0),
        contract_matrices(hidden_activation, backward_down_codes, 0, 0),
        adapter_scale * contract_matrices(down_rank_codes, token_partial_rows, 0, 0),
    )
    out_pairs = collect(out_part, slot_map, experts, capacity).reshape(tok_count, 2, -1)
    mixed_out = jnp.sum(out_pairs * router_gate_weights[:, :, None], axis=1).astype(jnp.bfloat16)
    prob_terms = jnp.sum(out_pairs * output_gradient[:, None, :].astype(jnp.float32), axis=2)
    prob_grads = lax.psum(prob_terms, ("tensor", "dp"))
    dx_pairs = collect(dx_part, slot_map, experts, capacity).reshape(tok_count, 2, -1)
    grad_tokens = jnp.sum(dx_pairs, axis=1).astype(jnp.bfloat16)
    return (
        mixed_out,
        grad_tokens,
        prob_grads,
        grad_list[0][None],
        grad_list[1][None],
        grad_list[2][None],
        grad_list[3][None],
        grad_list[4][None],
        grad_list[5][None],
    )


def solution(mesh):
    in_specs = (
        P(("groups", "expert"), ("tensor", "dp")),
        P(("groups", "expert"), ("tensor", "dp")),
        P(("groups", "expert"), None),
        P(("groups", "expert"), None),
        P("expert", None, ("tensor", "dp")),
        P("expert", None, ("tensor", "dp")),
        P("expert", ("tensor", "dp"), None),
        P("expert", ("tensor", "dp"), None),
        P("expert", None, ("tensor", "dp")),
        P("expert", ("tensor", "dp"), None),
        P("expert", None, ("tensor", "dp")),
        P("expert", ("tensor", "dp"), None),
        P("expert", None, ("tensor", "dp")),
    )
    out_specs = (
        P(("groups", "expert"), ("tensor", "dp")),
        P(("groups", "expert"), ("tensor", "dp")),
        P(("groups", "expert"), None),
        P(("groups", "expert"), ("tensor", "dp"), None),
        P(("groups", "expert"), None, ("tensor", "dp")),
        P(("groups", "expert"), ("tensor", "dp"), None),
        P(("groups", "expert"), None, ("tensor", "dp")),
        P(("groups", "expert"), ("tensor", "dp"), None),
        P(("groups", "expert"), None, ("tensor", "dp")),
    )
    quad = mesh.shape["tensor"] == 2 and mesh.shape["dp"] == 2
    return jax.shard_map(
        quad_device if quad else per_device, mesh=mesh, in_specs=in_specs, out_specs=out_specs, check_vma=False
    )
```

```python
import jax
import jax.numpy as jnp
from jax import lax
from jax.experimental import pallas as pl
from jax.experimental.pallas import tpu as pltpu
from jax.sharding import PartitionSpec as P

adapter_scale = 2.0


def contract_matrices(left_op, right_op, left_dim, right_dim):
    return lax.dot_general(
        left_op,
        right_op,
        (((left_dim,), (right_dim,)), ((), ())),
        preferred_element_type=jnp.float32,
    )


def silu_parts(gate_preactivation):
    sig_val = jax.nn.sigmoid(gate_preactivation)
    return (gate_preactivation * sig_val, sig_val * (1.0 + gate_preactivation * (1.0 - sig_val)))


def build_table(chosen_expert_index, experts, capacity):
    flat_ids = chosen_expert_index.reshape(-1)
    hit_mask = (flat_ids[:, None] == jnp.arange(experts, dtype=jnp.int32)[None, :]).astype(
        jnp.int32
    )
    before = jnp.cumsum(hit_mask, axis=0) - hit_mask
    slot_num = jnp.sum(before * hit_mask, axis=1)
    target = flat_ids * capacity + slot_num
    return (target[:, None] == jnp.arange(experts * capacity, dtype=jnp.int32)[None, :]).astype(
        jnp.bfloat16
    )


def collect(results, slot_map, experts, capacity):
    returned = lax.all_to_all(
        results.reshape(experts, capacity, -1), "expert", split_axis=0, concat_axis=0, tiled=True
    )
    return contract_matrices(slot_map, returned.reshape(experts * capacity, -1), 1, 0)


def expert_forward(
    input_full_rows,
    gate_weight_matrix,
    up_weight_matrix,
    gate_output_factor,
    up_output_factor,
    gate_rank_codes,
    up_rank_codes,
):
    gate_preactivation = contract_matrices(
        input_full_rows, gate_weight_matrix, 1, 0
    ) + adapter_scale * contract_matrices(gate_rank_codes, gate_output_factor, 1, 0)
    up_preactivation = contract_matrices(
        input_full_rows, up_weight_matrix, 1, 0
    ) + adapter_scale * contract_matrices(up_rank_codes, up_output_factor, 1, 0)
    silu_val, silu_grad = silu_parts(gate_preactivation)
    hidden_activation = (silu_val * up_preactivation).astype(jnp.bfloat16)
    return (up_preactivation, silu_val, silu_grad, hidden_activation)


def expert_backward(
    token_full_rows,
    backward_down_codes,
    down_weight_matrix,
    down_input_factor,
    gate_weight_matrix,
    up_weight_matrix,
    gate_output_factor,
    up_output_factor,
    up_preactivation,
    silu_val,
    silu_grad,
):
    hidden_gradient = contract_matrices(
        token_full_rows, down_weight_matrix, 1, 1
    ) + contract_matrices(backward_down_codes, down_input_factor, 1, 1)
    gate_preact_gradient = (hidden_gradient * up_preactivation * silu_grad).astype(jnp.bfloat16)
    up_preact_gradient = (hidden_gradient * silu_val).astype(jnp.bfloat16)
    dx_terms = contract_matrices(
        gate_preact_gradient, gate_weight_matrix, 1, 1
    ) + contract_matrices(up_preact_gradient, up_weight_matrix, 1, 1)
    code_terms = (
        contract_matrices(gate_preact_gradient, gate_output_factor, 1, 1),
        contract_matrices(up_preact_gradient, up_output_factor, 1, 1),
    )
    return (gate_preact_gradient, up_preact_gradient, dx_terms, code_terms)


def flat_sum(partial_terms, extra_term):
    main_sum = lax.psum_scatter(partial_terms, ("tensor", "dp"), scatter_dimension=1, tiled=True)
    return (main_sum + extra_term).astype(jnp.bfloat16)


vmem_bytes = 48 * 1024 * 1024


def nn(left_op, right_op):
    return contract_matrices(left_op, right_op, 1, 0)


def nt(left_op, right_op):
    return contract_matrices(left_op, right_op, 1, 1)


def call_tiles(
    body, tiles, order, operands, in_specs, out_shape, out_specs, flops, moved, after=(), alias=0
):
    count, extra = len(operands), len(after)
    operands = (*operands, *after)
    in_specs = [*in_specs, *[pl.BlockSpec(memory_space=pl.ANY)] * extra]

    def inner(order_ref, *refs):
        body(order_ref, *refs[:count], *refs[count + extra :])

    return pl.pallas_call(
        inner,
        grid_spec=pltpu.PrefetchScalarGridSpec(
            num_scalar_prefetch=1, grid=(tiles,), in_specs=in_specs, out_specs=out_specs
        ),
        out_shape=out_shape,
        input_output_aliases={1 + count + a: a for a in range(alias)},
        compiler_params=pltpu.CompilerParams(vmem_limit_bytes=vmem_bytes),
        cost_estimate=pl.CostEstimate(flops=flops, bytes_accessed=moved, transcendentals=0),
    )(order, *operands)


def whole(arr):
    return pl.BlockSpec(arr.shape, lambda n, order: (0, 0))


def forward_tiles(
    order, pieces, gate_w, up_w, gate_codes, up_codes, gate_b, up_b, half, prior=(), after=(), tile=256
):
    rows, width = pieces[0].shape
    hidden = gate_w.shape[1]
    parts = len(pieces)
    steps = hidden // tile // 2
    base = half * steps

    def body(order_ref, *refs):
        xs, gs, us = refs[:parts], refs[parts : 2 * parts], refs[2 * parts : 3 * parts]
        gc, uc, gb, ub, hid_ref, up_ref, val_ref = refs[3 * parts :]
        gate = adapter_scale * nn(gc[...], gb[...])
        up = adapter_scale * nn(uc[...], ub[...])
        for x_ref, g_ref in zip(xs, gs):
            gate += nn(x_ref[...], g_ref[...])
        for x_ref, u_ref in zip(xs, us):
            up += nn(x_ref[...], u_ref[...])
        val, grad = silu_parts(gate)
        hid_ref[...] = (val * up).astype(jnp.bfloat16)
        up_ref[...] = up * grad
        val_ref[...] = val

    def weight(k):
        return pl.BlockSpec((width, tile), lambda n, order: (order[k], base + n))

    def column(arr):
        return pl.BlockSpec((arr.shape[0], tile), lambda n, order: (0, base + n))

    out = pl.BlockSpec((rows, tile), lambda n, order: (0, base + n))
    return call_tiles(
        body,
        steps,
        order,
        (*pieces, *[gate_w] * parts, *[up_w] * parts, gate_codes, up_codes, gate_b, up_b),
        [whole(p) for p in pieces]
        + [weight(k) for k in range(parts)] * 2
        + [whole(gate_codes), whole(up_codes), column(gate_b), column(up_b)],
        (
            jax.ShapeDtypeStruct((rows, hidden), jnp.bfloat16),
            jax.ShapeDtypeStruct((rows, hidden), jnp.float32),
            jax.ShapeDtypeStruct((rows, hidden), jnp.float32),
        ),
        (out, out, out),
        2 * rows * width * parts * hidden,
        2 * width * parts * hidden,
        (*prior, *after),
        len(prior),
    )


def backward_tiles(order, pieces, down_w, codes, down_a, up_term, silu_val, after=(), tile=256):
    rows, width = pieces[0].shape
    hidden = down_w.shape[0]
    parts = len(pieces)

    def body(order_ref, *refs):
        ts, ws = refs[:parts], refs[parts : 2 * parts]
        bc, da, up_ref, val_ref, dg_ref, du_ref = refs[2 * parts :]
        grad = nt(bc[...], da[...])
        for t_ref, w_ref in zip(ts, ws):
            grad += nt(t_ref[...], w_ref[...])
        dg_ref[...] = (grad * up_ref[...]).astype(jnp.bfloat16)
        du_ref[...] = (grad * val_ref[...]).astype(jnp.bfloat16)

    def weight(k):
        return pl.BlockSpec((tile, width), lambda n, order: (n, order[k]))

    out = pl.BlockSpec((rows, tile), lambda n, order: (0, n))
    return call_tiles(
        body,
        hidden // tile,
        order,
        (*pieces, *[down_w] * parts, codes, down_a, up_term, silu_val),
        [whole(p) for p in pieces]
        + [weight(k) for k in range(parts)]
        + [whole(codes), pl.BlockSpec((tile, down_a.shape[1]), lambda n, order: (n, 0)), out, out],
        (jax.ShapeDtypeStruct((rows, hidden), jnp.bfloat16),) * 2,
        (out, out),
        2 * rows * width * parts * hidden,
        2 * width * parts * hidden,
        after,
    )


def feature_piece(order, k, left, weights, transposed, width, added, kind, tile, after):
    rows, hidden = left[0].shape
    count = len(left)
    steps = width // tile

    def body(order_ref, *refs):
        total = None
        for l_ref, w_ref in zip(refs[:count], refs[count : 2 * count]):
            term = (nt if transposed else nn)(l_ref[...], w_ref[...])
            total = term if total is None else total + term
        if added is not None:
            total = total + refs[2 * count][...].astype(jnp.float32)
        refs[-1][...] = total.astype(kind)

    out = pl.BlockSpec((rows, tile), lambda n, order: (0, n))
    if transposed:
        weight = pl.BlockSpec((tile, hidden), lambda n, order: (order[k] * steps + n, 0))
    else:
        weight = pl.BlockSpec((hidden, tile), lambda n, order: (0, order[k] * steps + n))
    extra = () if added is None else (added,)
    return call_tiles(
        body,
        steps,
        order,
        (*left, *weights, *extra),
        [whole(a) for a in left] + [weight] * count + [out] * len(extra),
        jax.ShapeDtypeStruct((rows, width), kind),
        out,
        2 * rows * hidden * width * count,
        2 * hidden * width * count,
        after,
    )


def stack_rows(blocks, order, after):
    height, width = blocks[0].shape

    def body(order_ref, *refs):
        for b, ref in enumerate(refs[:-1]):
            refs[-1][b * height : (b + 1) * height, :] = ref[...]

    shape = (height * len(blocks), width)
    return call_tiles(
        body,
        1,
        order,
        blocks,
        [whole(b) for b in blocks],
        jax.ShapeDtypeStruct(shape, blocks[0].dtype),
        pl.BlockSpec(shape, lambda n, order: (0, 0)),
        0,
        4 * shape[0] * width,
        after,
    )


def add_block(kept, extra, met, s, order, after):
    def body(order_ref, kept_ref, extra_ref, met_ref, out_ref):
        total = kept_ref[...] + extra_ref[...] + met_ref[...].astype(jnp.float32)
        out_ref[...] = total.astype(jnp.bfloat16)

    rows = pl.BlockSpec(met.shape, lambda n, order: (s, 0))
    return call_tiles(
        body,
        1,
        order,
        (kept, extra, met),
        [rows, rows, whole(met)],
        jax.ShapeDtypeStruct(met.shape, jnp.bfloat16),
        whole(met),
        0,
        12 * met.shape[0] * met.shape[1],
        after,
    )


def swap(arr, axis):
    return lax.ppermute(arr, axis, [(0, 1), (1, 0)])


def sum_pairs(arr):
    arr = arr + swap(arr, "dp")
    return arr + swap(arr, "tensor")


def rotate(arr, shift, experts):
    if shift % experts == 0:
        return arr
    return lax.ppermute(arr, "expert", [(e, (e + shift) % experts) for e in range(experts)])


def quad_device(
    tokens,
    output_gradient,
    chosen_expert_index,
    router_gate_weights,
    gate_frozen_weight,
    up_frozen_weight,
    down_frozen_weight,
    gate_adapter_input,
    gate_adapter_output,
    up_adapter_input,
    up_adapter_output,
    down_adapter_input,
    down_adapter_output,
):
    experts = lax.axis_size("expert")
    me = lax.axis_index("expert")
    tok_count, width = tokens.shape
    capacity = max(5 * tok_count // 8, 2 * tok_count // experts)
    buffer_rows = experts * capacity
    far, near = lax.axis_index("tensor"), lax.axis_index("dp")
    order = jnp.stack(
        [2 * far + near, 2 * far + 1 - near, 2 * (1 - far) + near, 2 * (1 - far) + 1 - near]
    ).astype(jnp.int32)
    gate_w, up_w, down_w = gate_frozen_weight[0], up_frozen_weight[0], down_frozen_weight[0]
    gate_a, up_a, down_a = gate_adapter_input[0], up_adapter_input[0], down_adapter_input[0]
    gate_b, up_b, down_b = gate_adapter_output[0], up_adapter_output[0], down_adapter_output[0]

    hits = [
        chosen_expert_index[:, k : k + 1] == jnp.arange(experts, dtype=jnp.int32)[None, :]
        for k in range(2)
    ]
    both = (hits[0] | hits[1]).astype(jnp.bfloat16)
    place = jnp.arange(tok_count, dtype=jnp.int32)
    earlier = (place[:, None] > place[None, :]).astype(jnp.bfloat16)
    before = nn(earlier, both).astype(jnp.int32)
    slot_maps = []
    for k in range(2):
        slot_num = jnp.sum(jnp.where(hits[k], before, 0), axis=1)
        turned = lax.rem(chosen_expert_index[:, k] - me + experts, experts)
        target = turned * capacity + slot_num
        slot_maps.append(
            (target[:, None] == jnp.arange(buffer_rows, dtype=jnp.int32)[None, :]).astype(
                jnp.bfloat16
            )
        )
    token_map = slot_maps[0] + slot_maps[1]
    gradient_wide = output_gradient.astype(jnp.float32)
    probs = [router_gate_weights[:, k : k + 1] for k in range(2)]

    def to_experts(buf):
        cut = [buf[s * capacity : (s + 1) * capacity] for s in range(experts)]
        return [rotate(cut[s], s, experts) for s in range(experts)]

    def across(blocks):
        return jnp.concatenate([swap(block, "tensor") for block in blocks])

    rank = gate_a.shape[1]
    code_factor = jnp.concatenate([gate_a, up_a], axis=1)
    code_far = swap(code_factor, "tensor")
    code_factors = (code_factor, swap(code_factor, "dp"), code_far, swap(code_far, "dp"))

    x_buf = contract_matrices(token_map, tokens, 0, 0).astype(jnp.bfloat16)
    t_buf = (
        contract_matrices(slot_maps[0], (gradient_wide * probs[0]).astype(jnp.bfloat16), 0, 0)
        + contract_matrices(slot_maps[1], (gradient_wide * probs[1]).astype(jnp.bfloat16), 0, 0)
    ).astype(jnp.bfloat16)
    x_blocks = to_experts(x_buf)
    x_part, x_far = jnp.concatenate(x_blocks), across(x_blocks)
    x_pieces = (x_part, swap(x_part, "dp"), x_far, swap(x_far, "dp"))
    t_blocks = to_experts(stack_rows((t_buf,), order, x_blocks))

    codes = sum(nn(x, a) for x, a in zip(x_pieces, code_factors)).astype(jnp.bfloat16)
    gate_codes, up_codes = codes[:, :rank], codes[:, rank:]

    forward_args = (order, x_pieces, gate_w, up_w, gate_codes, up_codes, gate_b, up_b)
    first_half = forward_tiles(*forward_args, 0)
    t_part = stack_rows(t_blocks, order, first_half[:1])
    t_far = across([t_part[s * capacity : (s + 1) * capacity] for s in range(experts)])
    t_pieces = (t_part, swap(t_part, "dp"), t_far, swap(t_far, "dp"))
    back_down = (adapter_scale * sum_pairs(nt(t_part, down_b))).astype(jnp.bfloat16)
    hidden_act, up_term, silu_val = forward_tiles(*forward_args, 1, first_half, (t_part,))

    def out_piece(k, added, kind, after):
        return feature_piece(order, k, (hidden_act,), (down_w,), False, width, added, kind, 512, after)

    def meet(to_chip):
        return [
            swap(to_chip[s * capacity : (s + 1) * capacity], "tensor") for s in range(experts)
        ]

    def send_back(kept, met, extra, gate):
        arrived = {}
        for s in [*range(2, experts), 1, 0]:
            gate = add_block(kept, extra, met[s], s, order, (gate,))
            arrived[s] = rotate(gate, -s, experts)
        return [arrived[s] for s in range(experts)]

    out_3 = out_piece(3, None, jnp.bfloat16, (t_far,))
    out_1 = out_piece(1, None, jnp.bfloat16, (out_3,))
    down_codes = sum_pairs(nn(hidden_act, down_a)).astype(jnp.bfloat16)
    d_gate, d_up = backward_tiles(
        order, t_pieces, down_w, back_down, down_a, up_term, silu_val, (out_1,)
    )
    out_chip = out_piece(2, swap(out_3, "dp"), jnp.bfloat16, (d_gate,))
    out_kept = out_piece(0, swap(out_1, "dp"), jnp.float32, (out_chip,))
    out_met = meet(out_chip)

    def dx_piece(k, added, kind, after):
        return feature_piece(
            order, k, (d_gate, d_up), (gate_w, up_w), True, width, added, kind, 256, after
        )

    dx_3 = dx_piece(3, None, jnp.bfloat16, (out_kept,))
    dx_1 = dx_piece(1, None, jnp.bfloat16, (dx_3,))
    dx_chip = dx_piece(2, swap(dx_3, "dp"), jnp.bfloat16, (dx_1, *out_met))
    out_back = send_back(out_kept, out_met, adapter_scale * nn(down_codes, down_b), dx_3)
    dx_kept = dx_piece(0, swap(dx_1, "dp"), jnp.float32, (dx_chip,))
    back_codes = adapter_scale * sum_pairs(
        jnp.concatenate([nt(d_gate, gate_b), nt(d_up, up_b)], axis=1)
    )
    back_codes = back_codes.astype(jnp.bfloat16)
    back_gate, back_up = back_codes[:, :rank], back_codes[:, rank:]
    dx_extra = nt(back_gate, gate_a) + nt(back_up, up_a)
    out_back = stack_rows(out_back, order, (dx_chip,))
    dx_back = jnp.concatenate(send_back(dx_kept, meet(dx_chip), dx_extra, dx_kept))

    grad_codes = contract_matrices(x_part, back_codes, 0, 0)
    grad_list = (
        grad_codes[:, :rank],
        adapter_scale * contract_matrices(gate_codes, d_gate, 0, 0),
        grad_codes[:, rank:],
        adapter_scale * contract_matrices(up_codes, d_up, 0, 0),
        contract_matrices(hidden_act, back_down, 0, 0),
        adapter_scale * contract_matrices(down_codes, t_part, 0, 0),
    )
    rows_out = [nn(slot_maps[k], out_back) for k in range(2)]
    mixed_out = (rows_out[0] * probs[0] + rows_out[1] * probs[1]).astype(jnp.bfloat16)
    prob_grads = sum_pairs(
        jnp.stack([jnp.sum(rows_out[k] * gradient_wide, axis=1) for k in range(2)], axis=1)
    )
    grad_tokens = nn(token_map, dx_back).astype(jnp.bfloat16)
    return (mixed_out, grad_tokens, prob_grads, *[g[None] for g in grad_list])


def per_device(
    tokens,
    output_gradient,
    chosen_expert_index,
    router_gate_weights,
    gate_frozen_weight,
    up_frozen_weight,
    down_frozen_weight,
    gate_adapter_input,
    gate_adapter_output,
    up_adapter_input,
    up_adapter_output,
    down_adapter_input,
    down_adapter_output,
):
    experts = lax.axis_size("expert")
    tok_count = tokens.shape[0]
    capacity = max(5 * tok_count // 8, 2 * tok_count // experts)
    buffer_rows = experts * capacity
    slot_map = build_table(chosen_expert_index, experts, capacity)
    probs_flat = router_gate_weights.reshape(-1, 1)
    gate_weight_matrix = gate_frozen_weight[0]
    up_weight_matrix = up_frozen_weight[0]
    down_weight_matrix = down_frozen_weight[0]
    gate_input_factor = gate_adapter_input[0]
    gate_output_factor = gate_adapter_output[0]
    up_input_factor = up_adapter_input[0]
    up_output_factor = up_adapter_output[0]
    down_input_factor = down_adapter_input[0]
    down_output_factor = down_adapter_output[0]
    t_rows = (jnp.repeat(output_gradient, 2, axis=0).astype(jnp.float32) * probs_flat).astype(
        jnp.bfloat16
    )
    x_buf = (
        contract_matrices(slot_map, jnp.repeat(tokens, 2, axis=0), 0, 0)
        .astype(jnp.bfloat16)
        .reshape(experts, capacity, -1)
    )
    t_buf = (
        contract_matrices(slot_map, t_rows, 0, 0)
        .astype(jnp.bfloat16)
        .reshape(experts, capacity, -1)
    )
    x_arrived, t_arrived = (
        lax.all_to_all(x_buf, "expert", split_axis=0, concat_axis=0, tiled=True),
        lax.all_to_all(t_buf, "expert", split_axis=0, concat_axis=0, tiled=True),
    )
    x_part = x_arrived.reshape(buffer_rows, -1)
    token_partial_rows = t_arrived.reshape(buffer_rows, -1)
    rank_code_totals = lax.psum(
        (
            contract_matrices(x_part, gate_input_factor, 1, 0),
            contract_matrices(x_part, up_input_factor, 1, 0),
            contract_matrices(token_partial_rows, down_output_factor, 1, 1),
        ),
        ("tensor", "dp"),
    )
    gate_rank_codes = rank_code_totals[0].astype(jnp.bfloat16)
    up_rank_codes = rank_code_totals[1].astype(jnp.bfloat16)
    backward_down_codes = (adapter_scale * rank_code_totals[2]).astype(jnp.bfloat16)
    input_full_rows, token_full_rows = (
        lax.all_gather(x_part, ("tensor", "dp"), axis=1, tiled=True),
        lax.all_gather(token_partial_rows, ("tensor", "dp"), axis=1, tiled=True),
    )
    up_preactivation, silu_val, silu_grad, hidden_activation = expert_forward(
        input_full_rows,
        gate_weight_matrix,
        up_weight_matrix,
        gate_output_factor,
        up_output_factor,
        gate_rank_codes,
        up_rank_codes,
    )
    down_rank_codes = lax.psum(
        contract_matrices(hidden_activation, down_input_factor, 1, 0), ("tensor", "dp")
    ).astype(jnp.bfloat16)
    out_part = flat_sum(
        contract_matrices(hidden_activation, down_weight_matrix, 1, 0),
        adapter_scale * contract_matrices(down_rank_codes, down_output_factor, 1, 0),
    )
    gate_preact_gradient, up_preact_gradient, dx_terms, code_terms = expert_backward(
        token_full_rows,
        backward_down_codes,
        down_weight_matrix,
        down_input_factor,
        gate_weight_matrix,
        up_weight_matrix,
        gate_output_factor,
        up_output_factor,
        up_preactivation,
        silu_val,
        silu_grad,
    )
    backward_rank_codes = lax.psum((code_terms[0], code_terms[1]), ("tensor", "dp"))
    gate_code_gradient = (adapter_scale * backward_rank_codes[0]).astype(jnp.bfloat16)
    up_code_gradient = (adapter_scale * backward_rank_codes[1]).astype(jnp.bfloat16)
    dx_part = flat_sum(
        dx_terms,
        contract_matrices(gate_code_gradient, gate_input_factor, 1, 1)
        + contract_matrices(up_code_gradient, up_input_factor, 1, 1),
    )
    grad_list = (
        contract_matrices(x_part, gate_code_gradient, 0, 0),
        adapter_scale * contract_matrices(gate_rank_codes, gate_preact_gradient, 0, 0),
        contract_matrices(x_part, up_code_gradient, 0, 0),
        adapter_scale * contract_matrices(up_rank_codes, up_preact_gradient, 0, 0),
        contract_matrices(hidden_activation, backward_down_codes, 0, 0),
        adapter_scale * contract_matrices(down_rank_codes, token_partial_rows, 0, 0),
    )
    out_pairs = collect(out_part, slot_map, experts, capacity).reshape(tok_count, 2, -1)
    mixed_out = jnp.sum(out_pairs * router_gate_weights[:, :, None], axis=1).astype(jnp.bfloat16)
    prob_terms = jnp.sum(out_pairs * output_gradient[:, None, :].astype(jnp.float32), axis=2)
    prob_grads = lax.psum(prob_terms, ("tensor", "dp"))
    dx_pairs = collect(dx_part, slot_map, experts, capacity).reshape(tok_count, 2, -1)
    grad_tokens = jnp.sum(dx_pairs, axis=1).astype(jnp.bfloat16)
    return (
        mixed_out,
        grad_tokens,
        prob_grads,
        grad_list[0][None],
        grad_list[1][None],
        grad_list[2][None],
        grad_list[3][None],
        grad_list[4][None],
        grad_list[5][None],
    )


def solution(mesh):
    in_specs = (
        P(("groups", "expert"), ("tensor", "dp")),
        P(("groups", "expert"), ("tensor", "dp")),
        P(("groups", "expert"), None),
        P(("groups", "expert"), None),
        P("expert", None, ("tensor", "dp")),
        P("expert", None, ("tensor", "dp")),
        P("expert", ("tensor", "dp"), None),
        P("expert", ("tensor", "dp"), None),
        P("expert", None, ("tensor", "dp")),
        P("expert", ("tensor", "dp"), None),
        P("expert", None, ("tensor", "dp")),
        P("expert", ("tensor", "dp"), None),
        P("expert", None, ("tensor", "dp")),
    )
    out_specs = (
        P(("groups", "expert"), ("tensor", "dp")),
        P(("groups", "expert"), ("tensor", "dp")),
        P(("groups", "expert"), None),
        P(("groups", "expert"), ("tensor", "dp"), None),
        P(("groups", "expert"), None, ("tensor", "dp")),
        P(("groups", "expert"), ("tensor", "dp"), None),
        P(("groups", "expert"), None, ("tensor", "dp")),
        P(("groups", "expert"), ("tensor", "dp"), None),
        P(("groups", "expert"), None, ("tensor", "dp")),
    )
    quad = mesh.shape["tensor"] == 2 and mesh.shape["dp"] == 2
    return jax.shard_map(
        quad_device if quad else per_device, mesh=mesh, in_specs=in_specs, out_specs=out_specs, check_vma=False
    )
```
